32 devices in a mesh: groups: 2 (over y), space: 4 (over z), tm: 2 (over x), probe: 2 (over core).
Axes of the slice: x: 2, y: 2, z: 4, core: 2. Of those that a mesh axis runs over, the one named last changes fastest.
Arguments:
- points: float32 [16, 32, 3, 256], P(('groups', 'space'), 'tm'), parts along dimension 0, may hold values from 0 to 512, as said below
- probes: bfloat16 [16, 32, 8, 256], P(('groups', 'space'), 'tm', 'probe'), parts along dimension 0, may hold values from -6 to 6
- basis: bfloat16 [16, 32, 64, 256], P(('groups', 'space'), 'tm'), parts along dimension 0, may hold values from -0.375 to 0.375
- transfer: bfloat16 [16, 32, 64, 64], P(('groups', 'space'), 'tm'), parts along dimension 0, may hold values from -0.5 to 0.5
- coupling0: bfloat16 [16, 32, 12, 64, 64], P(('groups', 'space'), 'tm'), parts along dimension 0, may hold values from -0.21875 to 0.21875
- list0: int32 [16, 32, 12], P(('groups', 'space'), 'tm'), parts along dimension 0, may hold values from -1 to 255, as said below
- coupling1: bfloat16 [8, 2, 6, 64, 64], P(('groups', 'space'), 'tm'), parts along dimension 0, may hold values from -0.3125 to 0.3125
- list1: int32 [8, 2, 6], P(('groups', 'space'), 'tm'), parts along dimension 0, may hold values from -1 to 7, as said below
- near: int32 [16, 32, 9], P(('groups', 'space'), 'tm'), parts along dimension 0, may hold values from 0 to 255, as said below
Outputs:
- product: float32 [16, 32, 8, 256], P(('groups', 'space'), 'tm', 'probe'), parts along dimension 0
The draws below stay inside these ranges and needn't reach their ends.
There are 2 independent parts, one for each index of `groups`. The reference program is written for one: setup_inputs(seed, part) draws one part's arguments, and reference() takes and returns one part's arrays. A program takes and returns all parts, laid end to end along the dimension named above; each array names one. Nothing has to cross between parts.
Inputs may be any that keep to these rules, and one draw needn't show every extreme that they name: `points`: leaf (a, b) has its first coordinate in [a 16, (a + 1) * 16), its second in [0, 32), its third in [b * 16, (b + 1) * 16). `near`: the 9 entries of leaf (a, b) are distinct leaves (a2, b2) with |a2 - a| <= 2 and |b2 - b| <= 2. `list0`: -1 pads. Other entries of leaf (a, b) are distinct leaves (a2, b2) with |a2 - a| <= 5 and |b2 - b| <= 5, and |a2 - a| > 2 or |b2 - b| > 2; each leaf has 6 to 12 of them. `list1`: -1 pads. Other entries are distinct nodes other than the node itself; each node has 3 to 6 of them.
All inputs are finite; a program needn't handle non-finite values.
Results may differ from the reference program's by a relative error of at most 0.0044.
Values may be sent and summed in bfloat16 or wider, within the bound.
A program may use at most 64 MiB of HBM per device.

```python
import jax
import jax.numpy as jnp
import numpy as np
from jax import lax

P_SIZE = 256
K = 64
R = 8
LS = 2
LT = 16
M0 = 12
M1 = 6
REACH = 5
CELL = 16
NA = 8
NB = 32
N_SPACE = 4
N_TM = 2


def pick_offsets(key, radius, inner, count):
    span = 2 * radius + 1
    off_a = jnp.array(np.repeat(np.arange(-radius, radius + 1), span), dtype=jnp.int32)
    off_b = jnp.array(np.tile(np.arange(-radius, radius + 1), span), dtype=jnp.int32)
    row_a = jnp.arange(NA, dtype=jnp.int32)[:, None, None] + off_a
    row_b = jnp.arange(NB, dtype=jnp.int32)[None, :, None] + off_b
    valid = (row_a >= 0) & (row_a < NA) & (row_b >= 0) & (row_b < NB)
    valid = valid & (jnp.maximum(jnp.abs(off_a), jnp.abs(off_b)) > inner)
    scores = jax.random.randint(key, (NA, NB, span * span), 0, 1 << 20) * 256 + jnp.arange(span * span, dtype=jnp.int32)
    scores = jnp.where(valid, scores, 1 << 30)
    order = jnp.argsort(scores, axis=-1, stable=True)[..., :count]
    ids = row_a * NB + row_b
    return jnp.take_along_axis(ids, order, axis=-1).astype(jnp.int32)


def draw_points(key, part):
    key = jax.random.fold_in(key, 11)
    first, second, third = jax.random.split(key, 3)
    row_a = jnp.arange(NA, dtype=jnp.float32)[:, None, None]
    row_b = jnp.arange(NB, dtype=jnp.float32)[None, :, None]
    east = (row_a + jax.random.uniform(first, (NA, NB, P_SIZE), jnp.float32)) * CELL
    north = jax.random.uniform(second, (NA, NB, P_SIZE), jnp.float32) * (2.0 * CELL)
    hours = (row_b + jax.random.uniform(third, (NA, NB, P_SIZE), jnp.float32)) * CELL
    return jnp.stack([east, north, hours], axis=2).astype(jnp.float32)


def draw_near(key, part):
    key = jax.random.fold_in(key, 12)
    return pick_offsets(key, 2, -1, 9)


def draw_list0(key, part):
    key = jax.random.fold_in(key, 13)
    first, second = jax.random.split(key)
    ids = pick_offsets(first, REACH, 2, M0)
    filled = jax.random.randint(second, (NA, NB, 1), M0 // 2, M0 + 1)
    return jnp.where(jnp.arange(M0, dtype=jnp.int32) < filled, ids, -1).astype(jnp.int32)


def draw_list1(key, part):
    key = jax.random.fold_in(key, 14)
    first, second = jax.random.split(key)
    nodes = N_SPACE * N_TM
    own = (jnp.arange(N_SPACE, dtype=jnp.int32)[:, None] * N_TM + jnp.arange(N_TM, dtype=jnp.int32)[None, :])[..., None]
    everyone = jnp.arange(nodes, dtype=jnp.int32)
    scores = jax.random.randint(first, (N_SPACE, N_TM, nodes), 0, 1 << 20) * 256 + everyone
    scores = jnp.where(everyone == own, 1 << 30, scores)
    order = jnp.argsort(scores, axis=-1, stable=True)[..., :M1].astype(jnp.int32)
    filled = jax.random.randint(second, (N_SPACE, N_TM, 1), M1 // 2, M1 + 1)
    return jnp.where(jnp.arange(M1, dtype=jnp.int32) < filled, order, -1).astype(jnp.int32)


def block_levels(own_key, shape, pieces, low, top_value):
    def one(position, parts):
        heights = jax.random.uniform(jax.random.fold_in(jax.random.fold_in(own_key, 6), position), (parts,), jnp.float32, low / len(pieces), top_value / len(pieces))
        return jnp.repeat(jnp.exp(heights), shape[position] // parts).reshape((-1,) + (1,) * (len(shape) - position - 1))

    factor_of = one(*pieces[0])
    for cut in pieces[1:]:
        factor_of = factor_of * one(*cut)
    return factor_of


def centred(rng, dims, width, limit, pieces=(), kind=jnp.bfloat16):
    factor_of = block_levels(rng, dims, pieces, -0.22, 0.18) if pieces else 1.0
    values = jax.random.normal(rng, dims, jnp.float32) * width * factor_of
    return jnp.minimum(jnp.maximum(values, -limit), limit).astype(kind)


def setup_inputs(seed: int = 0, part: int = 0) -> dict:
    key_of = jax.random.split(jax.random.key(seed), 10)
    part_splits = jax.random.split(jax.random.fold_in(key_of[9], part), 10)
    points = draw_points(jax.random.fold_in(jax.random.fold_in(key_of[9], part), 71), part)
    probes = centred(part_splits[1], (NA, NB, R, P_SIZE), 1.0, 6.0, ((0, 4), (1, 2), (2, 2)))
    basis = centred(part_splits[2], (NA, NB, K, P_SIZE), P_SIZE ** -0.5, 0.375, ((0, 4), (1, 2)))
    transfer = centred(part_splits[3], (NA, NB, K, K), (2 * K) ** -0.5, 0.5, ((0, 4), (1, 2)))
    coupling0 = centred(part_splits[4], (NA, NB, M0, K, K), (K * M0) ** -0.5, 0.21875, ((0, 4), (1, 2)))
    list0 = draw_list0(jax.random.fold_in(jax.random.fold_in(key_of[9], part), 71), part)
    coupling1 = centred(part_splits[6], (N_SPACE, N_TM, M1, K, K), (K * M1) ** -0.5, 0.3125, ((0, 4), (1, 2)))
    list1 = draw_list1(jax.random.fold_in(jax.random.fold_in(key_of[9], part), 71), part)
    near = draw_near(jax.random.fold_in(jax.random.fold_in(key_of[9], part), 71), part)
    return dict(points=points, probes=probes, basis=basis, transfer=transfer, coupling0=coupling0, list0=list0, coupling1=coupling1, list1=list1, near=near)


def kernel_block(own, other):
    space_rate = 1.0 / (4.5 * CELL * CELL)
    time_rate = 1.0 / (2.0 * CELL * CELL)
    near_own = own.astype(jnp.float32)
    far_other = other.astype(jnp.float32)
    east = near_own[..., 0, :, None] - far_other[..., 0, None, :]
    north = near_own[..., 1, :, None] - far_other[..., 1, None, :]
    hours = near_own[..., 2, :, None] - far_other[..., 2, None, :]
    value = 0.1 * jnp.exp(-(east * east + north * north) * space_rate - hours * hours * time_rate)
    return value.astype(jnp.bfloat16)


def reference(points, probes, basis, transfer, coupling0, list0, coupling1, list1, near):
    leaves = NA * NB
    coef = jnp.einsum('abrp,abkp->abrk', probes.astype(jnp.float32), basis.astype(jnp.float32)).astype(jnp.bfloat16)
    flat_pts = points.reshape(leaves, 3, P_SIZE)
    flat_prb = probes.reshape(leaves, R, P_SIZE)

    def near_row(pair):
        own, picks = pair
        other = flat_pts[picks]
        vectors = flat_prb[picks]
        kern = kernel_block(own[:, None], other)
        return jnp.einsum('bnpq,bnrq->brp', kern.astype(jnp.float32), vectors.astype(jnp.float32))

    near_part = lax.map(near_row, (points, near))
    coef_rows = coef.reshape(leaves, R * K)
    chosen = jnp.where(list0[..., None] >= 0, coef_rows[jnp.maximum(list0, 0)], 0)
    chosen = chosen.reshape(NA, NB, M0, R, K)
    level_zero = jnp.einsum('abmkq,abmrq->abrk', coupling0.astype(jnp.float32), chosen.astype(jnp.float32))
    upward = jnp.einsum('abkq,abrq->abrk', transfer.astype(jnp.float32), coef.astype(jnp.float32))
    node_coef = upward.reshape(N_SPACE, LS, N_TM, LT, R, K).sum(axis=(1, 3)).astype(jnp.bfloat16)
    node_rows = node_coef.reshape(N_SPACE * N_TM, R * K)
    chosen_nodes = jnp.where(list1[..., None] >= 0, node_rows[jnp.maximum(list1, 0)], 0)
    chosen_nodes = chosen_nodes.reshape(N_SPACE, N_TM, M1, R, K)
    level_one = jnp.einsum('stmkq,stmrq->strk', coupling1.astype(jnp.float32), chosen_nodes.astype(jnp.float32)).astype(jnp.bfloat16)
    spread = jnp.repeat(jnp.repeat(level_one, LS, axis=0), LT, axis=1)
    downward = jnp.einsum('abkq,abrk->abrq', transfer.astype(jnp.float32), spread.astype(jnp.float32))
    total = (level_zero + downward).astype(jnp.bfloat16)
    far_part = jnp.einsum('abrk,abkp->abrp', total.astype(jnp.float32), basis.astype(jnp.float32))
    return far_part + near_part
```

```python
import functools
import math

import jax
import jax.numpy as jnp
from jax import lax
from jax.experimental import pallas as pl
from jax.experimental.pallas import tpu as pltpu
from jax.sharding import PartitionSpec as P

CELL = 16
F32 = jnp.float32
BF16 = jnp.bfloat16
MESH = pl.DeviceIdType.MESH
LOG2E = math.log2(math.e)
SPACE_SCALE = math.sqrt(LOG2E / (4.5 * CELL * CELL))
TIME_SCALE = math.sqrt(LOG2E / (2.0 * CELL * CELL))
NODE_ROWS = 48

NT = (((1,), (1,)), ((), ()))


def dot(a, b, dims=(((1,), (0,)), ((), ()))):
    return lax.dot_general(a, b, dims, preferred_element_type=F32)


def split3(x):
    high = x.astype(BF16).astype(F32)
    rest = x - high
    mid = rest.astype(BF16).astype(F32)
    return high, mid, rest - mid


def kernel(
    n_space,
    n_tm,
    slots_ref,
    pack_ref,
    probes_ref,
    basis_ref,
    transfer_ref,
    coupling1_ref,
    rows_ref,
    coupling0_hbm,
    out_ref,
    win,
    other_feat,
    own_feat,
    vectors,
    near_mine,
    near_theirs,
    coef_f32,
    coef_send,
    piece,
    gathered,
    coupling0,
    halo_send,
    halo_recv,
    coef_ssem,
    coef_rsem,
    near_ssem,
    near_rsem,
    local_sem,
):
    space = lax.axis_index("space")
    tm = lax.axis_index("tm")
    core = lax.axis_index("probe")
    node = space * n_tm + tm
    nodes = n_space * n_tm
    leaves_a, leaves_b = basis_ref.shape[0], basis_ref.shape[1]
    count = leaves_a * leaves_b
    half = leaves_b // 2
    pairs = leaves_b // 2
    span = pairs // 2 + 1
    win_pairs = pairs // 2 + 2
    m0 = coupling0_hbm.shape[2]
    m1 = coupling1_ref.shape[2]
    rank = basis_ref.shape[2]

    load0 = pltpu.make_async_copy(coupling0_hbm, coupling0, local_sem.at[0])
    load0.start()

    barrier = pltpu.get_barrier_semaphore()

    def greet(k, carry):
        @pl.when(k != node * 2 + core)
        def _():
            pl.semaphore_signal(
                barrier,
                inc=1,
                device_id={
                    "space": k // (2 * n_tm),
                    "tm": (k // 2) % n_tm,
                    "probe": k % 2,
                },
                device_id_type=MESH,
            )

        return carry

    lax.fori_loop(0, 2 * nodes, greet, 0)
    pl.semaphore_wait(barrier, 2 * nodes - 1)

    def halo_pieces():
        for ds in (-1, 0, 1):
            for dt in (0, -1, 1):
                for to in (0, 1):
                    if dt == 1 and to == 1 or dt == -1 and to == 0:
                        continue
                    yield ds, dt, to

    def exists(ds, dt):
        s, t = space + ds, tm + dt
        return (s >= 0) & (s < n_space) & (t >= 0) & (t < n_tm)

    def halo_copy(ds, dt, to, source, s, t, c):
        if dt == 0:
            first, slot, length = 3 * to, 1 - to, span
        elif dt == 1:
            first, slot, length = pairs - 1, 0, 1
        else:
            first, slot, length = 0, win_pairs - 1, 1
        if dt == 0:
            first = (pairs // 2 - 1) * to
        return pltpu.make_async_remote_copy(
            src_ref=pack_ref.at[:, pl.ds(first, length)],
            dst_ref=win.at[source, pl.ds(2 - 2 * ds, 2), pl.ds(slot, length)],
            send_sem=halo_send.at[ds + 1, dt + 1, to],
            recv_sem=halo_recv.at[source, ds + 1, dt + 1],
            device_id={"space": s, "tm": t, "probe": c},
            device_id_type=MESH,
        )

    own_first = (pairs // 2 - 1) * core
    own_copy = pltpu.make_async_copy(
        pack_ref.at[:, pl.ds(own_first, span)],
        win.at[core, pl.ds(2, 2), pl.ds(1 - core, span)],
        local_sem.at[1],
    )
    own_copy.start()
    for ds, dt, to in halo_pieces():
        ok = exists(ds, dt)
        if ds == 0 and dt == 0:
            ok = core != to

        @pl.when(ok)
        def _(ds=ds, dt=dt, to=to):
            halo_copy(ds, dt, to, core, space + ds, tm + dt, to).start()

    node_sum = jnp.zeros((4, rank), F32)
    for i in range(count):
        a, b = i // leaves_b, i % leaves_b
        value = dot(probes_ref[a, b], basis_ref[a, b], NT).astype(BF16)
        node_sum = node_sum + dot(value, transfer_ref[a, b], NT)
        value = value.astype(F32)
        for r in range(4):
            coef_f32[r // 2, i, pl.ds((r % 2) * rank, rank)] = value[r]
    node_sum = node_sum.astype(BF16).astype(F32)
    for r in range(4):
        coef_f32[r // 2, count, pl.ds((r % 2) * rank, rank)] = node_sum[r]
    coef_f32[:, pl.ds(count + 1, NODE_ROWS - count - 1)] = jnp.zeros(
        (2, NODE_ROWS - count - 1, 2 * rank), F32
    )
    coef_send[...] = coef_f32[...].astype(BF16)

    def coef_copy(at, sem_at, to):
        return pltpu.make_async_remote_copy(
            src_ref=coef_send,
            dst_ref=piece.at[:, pl.ds(pl.multiple_of(at * NODE_ROWS, 16), NODE_ROWS)],
            send_sem=coef_ssem.at[sem_at],
            recv_sem=coef_rsem.at[at],
            device_id={"space": to // n_tm, "tm": to % n_tm, "probe": core},
            device_id_type=MESH,
        )

    def send_coef(k, carry):
        @pl.when(k != node)
        def _():
            coef_copy(node, k, k).start()

        return carry

    lax.fori_loop(0, nodes, send_coef, 0)
    own_coef = pltpu.make_async_copy(
        coef_send,
        piece.at[:, pl.ds(pl.multiple_of(node * NODE_ROWS, 16), NODE_ROWS)],
        local_sem.at[2],
    )
    own_coef.start()

    own_copy.wait()
    for source in (0, 1):
        for ds in (-1, 0, 1):
            for dt in (0, -1, 1):
                ok = exists(-ds, -dt)
                if dt == 1:
                    ok = ok & (core == 0)
                if dt == -1:
                    ok = ok & (core == 1)
                if ds == 0 and dt == 0:
                    ok = core != source

                if dt == 0:
                    for to in (0, 1):

                        @pl.when(ok & (core == to))
                        def _(ds=ds, dt=dt, to=to, source=source):
                            halo_copy(ds, dt, to, source, space, tm, core).wait_recv()
                else:

                    @pl.when(ok)
                    def _(ds=ds, dt=dt, source=source):
                        to = 0 if dt == 1 else 1
                        halo_copy(ds, dt, to, source, space, tm, core).wait_recv()

    row4 = lax.broadcasted_iota(jnp.int32, (4, 1), 0)
    scale = jnp.where(row4 == 2, TIME_SCALE, jnp.where(row4 == 3, 0.0, SPACE_SCALE))
    ones = jnp.where(lax.broadcasted_iota(jnp.int32, (4, 256), 0) < 3, 1.0, 0.0).astype(F32)
    zero1 = jnp.zeros((1, 256), F32)
    mid_a = (leaves_a + 4) / 2.0 - 0.5
    mid_b = (half + 4) / 2.0 - 0.5

    def features(w, j, carry):
        tiles = [win[s, w, j].astype(F32) for s in (0, 1)]
        for e in (0, 1):
            slot = (w * win_pairs + j) * 2 + e
            col = (j * 2 + e).astype(F32)
            place = jnp.where(
                row4 == 0,
                (w - mid_a) * CELL,
                jnp.where(row4 == 2, (col - mid_b) * CELL, 0.0),
            )
            at = (tiles[e][8:12] + tiles[e][12:16] + place) * scale
            high, mid, low = split3(at)
            norm = -jnp.sum(at * at, axis=0, keepdims=True)
            norms = jnp.concatenate([*split3(norm), zero1], axis=0)
            feat = jnp.concatenate([high, mid, low, high, mid, high, norms, ones], axis=0)
            other_feat[slot] = feat.astype(BF16)
            probe_rows = jnp.concatenate(
                [tiles[0][4 * e : 4 * e + 4], tiles[1][4 * e : 4 * e + 4]], axis=0
            )
            vectors[slot] = probe_rows.astype(BF16)
            if 2 <= w < 2 + leaves_a:
                norms = jnp.concatenate([*split3(norm + math.log2(0.1)), zero1], axis=0)
                high, mid, low = 2.0 * high, 2.0 * mid, 2.0 * low
                feat = jnp.concatenate([high, high, high, mid, mid, low, ones, norms], axis=0)
                own_feat[(w - 2) * win_pairs * 2 + j * 2 + e] = feat.T.astype(BF16)
        return carry

    for w in range(leaves_a + 4):
        lax.fori_loop(0, win_pairs, functools.partial(features, w), 0)

    picks = slots_ref.shape[0] // (leaves_a * half)

    def near_leaf(i, carry):
        own = own_feat[i // half * (2 * win_pairs) + i % half + 2]
        total = jnp.zeros((own.shape[0], 8), F32)
        for n in range(picks):
            slot = slots_ref[i * picks + n]
            kern = jnp.exp2(dot(own, other_feat[slot])).astype(BF16)
            total = total + dot(kern, vectors[slot], NT)
        near_mine[i] = total.T
        return carry

    lax.fori_loop(0, leaves_a * half, near_leaf, 0)

    near_copy = pltpu.make_async_remote_copy(
        src_ref=near_mine,
        dst_ref=near_theirs,
        send_sem=near_ssem,
        recv_sem=near_rsem,
        device_id={"probe": 1 - core},
        device_id_type=MESH,
    )
    near_copy.start()

    own_coef.wait()

    def take_coef(k, carry):
        @pl.when(k != node)
        def _():
            coef_copy(k, k, node).wait_recv()

        return carry

    lax.fori_loop(0, nodes, take_coef, 0)
    ids = rows_ref[...]
    hits = (
        lax.broadcasted_iota(jnp.int32, (ids.shape[0], nodes * NODE_ROWS), 1) == ids
    ).astype(BF16)
    for rp in (0, 1):
        chosen = dot(hits, piece[rp])
        gathered[2 * rp] = chosen[:, :rank].astype(BF16)
        gathered[2 * rp + 1] = chosen[:, rank:].astype(BF16)

    lane = lax.broadcasted_iota(jnp.int32, (rank, 64), 1)
    fold = (
        lax.broadcasted_iota(jnp.int32, (8, 64), 1) // 16
        == lax.broadcasted_iota(jnp.int32, (8, 64), 0)
    ).astype(BF16)

    def couple(blocks, row, length):
        probes4 = jnp.concatenate(
            [gathered[r, pl.ds(row, 16), :] for r in range(4)], axis=0
        )
        full = dot(blocks, probes4, NT)
        total = jnp.zeros((rank, 64), F32)
        for m in range(length):
            total = total + jnp.where(
                lane % 16 == m, full[m * rank : (m + 1) * rank], 0.0
            )
        high = total.astype(BF16)
        low = (total - high.astype(F32)).astype(BF16)
        return dot(fold, high, NT) + dot(fold, low, NT)

    load0.wait()
    level_one = couple(
        coupling1_ref[0, 0].reshape(m1 * rank, rank), count * 16, m1
    ).astype(BF16)

    def far_leaf(i, carry):
        a, b = i // leaves_b, i % leaves_b
        total = couple(
            coupling0[a, b].reshape(m0 * rank, rank), pl.multiple_of(i * 16, 16), m0
        )
        total = (total + dot(level_one, transfer_ref[a, b])).astype(BF16)
        out_ref[a, b] = dot(total, basis_ref[a, b])[:4]
        return carry

    lax.fori_loop(0, count, far_leaf, 0)

    near_copy.wait()

    def add_near(i, carry):
        a, b = i // half, i % half
        for refs, at in ((near_mine, core), (near_theirs, 1 - core)):
            value = refs[i]
            value = jnp.where(core == 0, value[:4], value[4:])
            out_ref[a, at * half + b] += value
        return carry

    lax.fori_loop(0, leaves_a * half, add_near, 0)

    for ds, dt, to in halo_pieces():
        ok = exists(ds, dt)
        if ds == 0 and dt == 0:
            ok = core != to

        @pl.when(ok)
        def _(ds=ds, dt=dt, to=to):
            halo_copy(ds, dt, to, core, space + ds, tm + dt, to).wait_send()

    def end_coef(k, carry):
        @pl.when(k != node)
        def _():
            coef_copy(node, k, k).wait_send()

        return carry

    lax.fori_loop(0, nodes, end_coef, 0)


def on_device(
    n_space, n_tm, points, probes, basis, transfer, coupling0, list0, coupling1, list1, near
):
    leaves_a, leaves_b, _, width = points.shape
    rank = basis.shape[2]
    count = leaves_a * leaves_b
    half = leaves_b // 2
    columns = leaves_b * n_tm
    nodes = n_space * n_tm
    space = lax.axis_index("space")
    tm = lax.axis_index("tm")
    core = lax.axis_index("probe")

    pair_points = points.reshape(leaves_a, leaves_b // 2, 2, 3, width)
    chosen = jnp.where(core == 0, pair_points[:, :, 0], pair_points[:, :, 1])
    east = (space * leaves_a + jnp.arange(leaves_a)).astype(F32)[:, None] * CELL + CELL / 2
    hour = (tm * leaves_b + core + 2 * jnp.arange(leaves_b // 2)).astype(F32)[
        None, :
    ] * CELL + CELL / 2
    shape = (leaves_a, leaves_b // 2)
    middle = jnp.stack(
        [jnp.broadcast_to(east, shape), jnp.full(shape, CELL, F32), jnp.broadcast_to(hour, shape)],
        axis=2,
    )
    local = chosen - middle[..., None]
    high = lax.reduce_precision(local, 8, 7)
    low = local - high
    gap = jnp.zeros((leaves_a, leaves_b // 2, 1, width), BF16)
    pack = jnp.concatenate(
        [
            probes.reshape(leaves_a, leaves_b // 2, 8, width),
            high.astype(BF16),
            gap,
            low.astype(BF16),
            gap,
        ],
        axis=2,
    )

    mine = lax.dynamic_slice_in_dim(near, core * half, half, axis=1)
    slots = (mine // columns - (space * leaves_a - 2)) * (half + 4) + (
        mine % columns - (tm * leaves_b + core * half - 2)
    )
    slots = slots.reshape(-1)

    row, column = list0 // columns, list0 % columns
    leaf_rows = (
        (row // leaves_a * n_tm + column // leaves_b) * NODE_ROWS
        + row % leaves_a * leaves_b
        + column % leaves_b
    )
    leaf_rows = jnp.where(list0 < 0, -1, leaf_rows).reshape(count, -1)
    leaf_rows = jnp.pad(leaf_rows, ((0, 0), (0, 16 - leaf_rows.shape[1])), constant_values=-1)
    node_rows = jnp.where(list1 < 0, -1, list1 * NODE_ROWS + count).reshape(1, -1)
    node_rows = jnp.pad(node_rows, ((0, 0), (0, 16 - node_rows.shape[1])), constant_values=-1)
    rows = jnp.concatenate([leaf_rows, node_rows], axis=0).reshape(-1, 1)

    win_pairs = half // 2 + 2
    window = (leaves_a + 4) * win_pairs * 2
    vmem = pl.BlockSpec(memory_space=pltpu.VMEM)
    return pl.pallas_call(
        functools.partial(kernel, n_space, n_tm),
        out_shape=jax.ShapeDtypeStruct(probes.shape, F32),
        in_specs=[pl.BlockSpec(memory_space=pltpu.SMEM)]
        + [vmem] * 6
        + [pl.BlockSpec(memory_space=pl.ANY)],
        out_specs=vmem,
        scratch_shapes=[
            pltpu.VMEM((2, leaves_a + 4, win_pairs, 16, width), BF16),
            pltpu.VMEM((window, 32, width), BF16),
            pltpu.VMEM((leaves_a * win_pairs * 2, width, 32), BF16),
            pltpu.VMEM((window, 8, width), BF16),
            pltpu.VMEM((leaves_a * half, 8, width), F32),
            pltpu.VMEM((leaves_a * half, 8, width), F32),
            pltpu.VMEM((2, NODE_ROWS, 2 * rank), F32),
            pltpu.VMEM((2, NODE_ROWS, 2 * rank), BF16),
            pltpu.VMEM((2, nodes * NODE_ROWS, 2 * rank), BF16),
            pltpu.VMEM((4, (count + 1) * 16, rank), BF16),
            pltpu.VMEM(coupling0.shape, BF16),
            pltpu.SemaphoreType.DMA((3, 3, 2)),
            pltpu.SemaphoreType.DMA((2, 3, 3)),
            pltpu.SemaphoreType.DMA((nodes,)),
            pltpu.SemaphoreType.DMA((nodes,)),
            pltpu.SemaphoreType.DMA,
            pltpu.SemaphoreType.DMA,
            pltpu.SemaphoreType.DMA((3,)),
        ],
        compiler_params=pltpu.CompilerParams(
            collective_id=0, has_side_effects=True, vmem_limit_bytes=48 * 1024 * 1024
        ),
    )(slots, pack, probes, basis, transfer, coupling1, rows, coupling0)


def solution(mesh):
    in_specs = (
        P(("groups", "space"), "tm", None, None),
        P(("groups", "space"), "tm", "probe", None),
        P(("groups", "space"), "tm", None, None),
        P(("groups", "space"), "tm", None, None),
        P(("groups", "space"), "tm", None, None, None),
        P(("groups", "space"), "tm", None),
        P(("groups", "space"), "tm", None, None, None),
        P(("groups", "space"), "tm", None),
        P(("groups", "space"), "tm", None),
    )
    out_specs = P(("groups", "space"), "tm", "probe", None)
    return jax.shard_map(
        functools.partial(on_device, mesh.shape["space"], mesh.shape["tm"]),
        mesh=mesh,
        in_specs=in_specs,
        out_specs=out_specs,
        check_vma=False,
    )
```

```python
import functools
import math

import jax
import jax.numpy as jnp
from jax import lax
from jax.experimental import pallas as pl
from jax.experimental.pallas import tpu as pltpu
from jax.sharding import PartitionSpec as P

CELL = 16
F32 = jnp.float32
BF16 = jnp.bfloat16
MESH = pl.DeviceIdType.MESH
LOG2E = math.log2(math.e)
SPACE_SCALE = math.sqrt(LOG2E / (4.5 * CELL * CELL))
TIME_SCALE = math.sqrt(LOG2E / (2.0 * CELL * CELL))
GROUP = 4
NODE_ROWS = 48

NT = (((1,), (1,)), ((), ()))


def dot(a, b, dims=(((1,), (0,)), ((), ()))):
    return lax.dot_general(a, b, dims, preferred_element_type=F32)


def split3(x):
    high = x.astype(BF16).astype(F32)
    rest = x - high
    mid = rest.astype(BF16).astype(F32)
    return high, mid, rest - mid


def kernel(
    n_space,
    n_tm,
    points_hbm,
    probes_hbm,
    basis_hbm,
    transfer_hbm,
    coupling0_hbm,
    list0_hbm,
    coupling1_hbm,
    list1_hbm,
    near_hbm,
    out_ref,
    points_ref,
    probes_ref,
    basis_ref,
    transfer_ref,
    coupling0,
    list0_ref,
    coupling1_ref,
    list1_ref,
    near_ref,
    pack_ref,
    ids_ref,
    hits_ref,
    win,
    other_feat,
    own_feat,
    vectors,
    near_mine,
    near_theirs,
    coef_f32,
    coef_send,
    piece,
    gathered,
    halo_send,
    halo_recv,
    coef_ssem,
    coef_rsem,
    near_ssem,
    near_rsem,
    local_sem,
):
    space = lax.axis_index("space")
    tm = lax.axis_index("tm")
    core = lax.axis_index("probe")
    node = space * n_tm + tm
    nodes = n_space * n_tm
    leaves_a, leaves_b = basis_ref.shape[0], basis_ref.shape[1]
    count = leaves_a * leaves_b
    half = leaves_b // 2
    pairs = leaves_b // 2
    span = pairs // 2 + 1
    win_pairs = pairs // 2 + 2
    m0 = coupling0_hbm.shape[2]
    m1 = coupling1_ref.shape[2]
    rank = basis_ref.shape[2]

    columns = leaves_b * n_tm
    loads = {}
    for at, (name, source, target) in enumerate(
        (
            ("points", points_hbm, points_ref),
            ("probes", probes_hbm, probes_ref),
            ("basis", basis_hbm, basis_ref),
            ("transfer", transfer_hbm, transfer_ref),
            ("list0", list0_hbm, list0_ref),
            ("list1", list1_hbm, list1_ref),
            ("near", near_hbm, near_ref),
            ("coupling1", coupling1_hbm, coupling1_ref),
            ("coupling0", coupling0_hbm, coupling0),
        )
    ):
        loads[name] = pltpu.make_async_copy(source, target, local_sem.at[at + 3])
        loads[name].start()

    barrier = pltpu.get_barrier_semaphore()

    def greet(k, carry):
        @pl.when(k != node * 2 + core)
        def _():
            pl.semaphore_signal(
                barrier,
                inc=1,
                device_id={
                    "space": k // (2 * n_tm),
                    "tm": (k // 2) % n_tm,
                    "probe": k % 2,
                },
                device_id_type=MESH,
            )

        return carry

    lax.fori_loop(0, 2 * nodes, greet, 0)

    loads["points"].wait()
    loads["probes"].wait()
    row3 = lax.broadcasted_iota(jnp.int32, (3, 1), 0)
    zero1 = jnp.zeros((1, 256), F32)
    for a in range(leaves_a):
        for j in range(pairs):
            east = ((space * leaves_a + a) * CELL + CELL // 2).astype(F32)
            hour = ((tm * leaves_b + 2 * j + core) * CELL + CELL // 2).astype(F32)
            middle = jnp.where(row3 == 0, east, jnp.where(row3 == 2, hour, float(CELL)))
            at = points_ref[a, 2 * j + core] - middle
            high = at.astype(BF16).astype(F32)
            tile = jnp.concatenate(
                [
                    probes_ref[a, 2 * j].astype(F32),
                    probes_ref[a, 2 * j + 1].astype(F32),
                    high,
                    zero1,
                    at - high,
                    zero1,
                ],
                axis=0,
            )
            pack_ref[a, j] = tile.astype(BF16)
    pl.semaphore_wait(barrier, 2 * nodes - 1)

    def halo_pieces():
        for ds in (-1, 0, 1):
            for dt in (0, -1, 1):
                for to in (0, 1):
                    if dt == 1 and to == 1 or dt == -1 and to == 0:
                        continue
                    yield ds, dt, to

    def exists(ds, dt):
        s, t = space + ds, tm + dt
        return (s >= 0) & (s < n_space) & (t >= 0) & (t < n_tm)

    def halo_copy(ds, dt, to, source, s, t, c):
        if dt == 0:
            first, slot, length = 3 * to, 1 - to, span
        elif dt == 1:
            first, slot, length = pairs - 1, 0, 1
        else:
            first, slot, length = 0, win_pairs - 1, 1
        if dt == 0:
            first = (pairs // 2 - 1) * to
        return pltpu.make_async_remote_copy(
            src_ref=pack_ref.at[:, pl.ds(first, length)],
            dst_ref=win.at[source, pl.ds(2 - 2 * ds, 2), pl.ds(slot, length)],
            send_sem=halo_send.at[ds + 1, dt + 1, to],
            recv_sem=halo_recv.at[source, ds + 1, dt + 1],
            device_id={"space": s, "tm": t, "probe": c},
            device_id_type=MESH,
        )

    own_first = (pairs // 2 - 1) * core
    own_copy = pltpu.make_async_copy(
        pack_ref.at[:, pl.ds(own_first, span)],
        win.at[core, pl.ds(2, 2), pl.ds(1 - core, span)],
        local_sem.at[1],
    )
    own_copy.start()
    for ds, dt, to in halo_pieces():
        ok = exists(ds, dt)
        if ds == 0 and dt == 0:
            ok = core != to

        @pl.when(ok)
        def _(ds=ds, dt=dt, to=to):
            halo_copy(ds, dt, to, core, space + ds, tm + dt, to).start()

    loads["basis"].wait()
    loads["transfer"].wait()
    node_sum = jnp.zeros((4, rank), F32)
    for i in range(count):
        a, b = i // leaves_b, i % leaves_b
        value = dot(probes_ref[a, b], basis_ref[a, b], NT).astype(BF16)
        node_sum = node_sum + dot(value, transfer_ref[a, b], NT)
        value = value.astype(F32)
        for r in range(4):
            coef_f32[r // 2, i, pl.ds((r % 2) * rank, rank)] = value[r]
    node_sum = node_sum.astype(BF16).astype(F32)
    for r in range(4):
        coef_f32[r // 2, count, pl.ds((r % 2) * rank, rank)] = node_sum[r]
    coef_f32[:, pl.ds(count + 1, NODE_ROWS - count - 1)] = jnp.zeros(
        (2, NODE_ROWS - count - 1, 2 * rank), F32
    )
    coef_send[...] = coef_f32[...].astype(BF16)

    def coef_copy(at, sem_at, to):
        return pltpu.make_async_remote_copy(
            src_ref=coef_send,
            dst_ref=piece.at[:, pl.ds(pl.multiple_of(at * NODE_ROWS, 16), NODE_ROWS)],
            send_sem=coef_ssem.at[sem_at],
            recv_sem=coef_rsem.at[at],
            device_id={"space": to // n_tm, "tm": to % n_tm, "probe": core},
            device_id_type=MESH,
        )

    def send_coef(k, carry):
        @pl.when(k != node)
        def _():
            coef_copy(node, k, k).start()

        return carry

    lax.fori_loop(0, nodes, send_coef, 0)
    own_coef = pltpu.make_async_copy(
        coef_send,
        piece.at[:, pl.ds(pl.multiple_of(node * NODE_ROWS, 16), NODE_ROWS)],
        local_sem.at[2],
    )
    own_coef.start()

    loads["list0"].wait()
    loads["list1"].wait()
    ids_ref[...] = jnp.full(ids_ref.shape, -1.0, F32)
    for a in range(leaves_a):
        named = list0_ref[a]
        row, column = named // columns, named % columns
        place = (
            (row // leaves_a * n_tm + column // leaves_b) * NODE_ROWS
            + row % leaves_a * leaves_b
            + column % leaves_b
        )
        ids_ref[a, :, pl.ds(0, m0)] = jnp.where(named < 0, -1, place).astype(F32)
    named = list1_ref[0]
    ids_ref[leaves_a, pl.ds(0, 1), pl.ds(0, m1)] = jnp.where(
        named < 0, -1, named * NODE_ROWS + count
    ).astype(F32)
    spread = lax.broadcasted_iota(jnp.int32, (16, nodes * NODE_ROWS), 1).astype(F32)
    for a in range(leaves_a + 1):
        turned = ids_ref[a].T
        for b in range(leaves_b if a < leaves_a else 1):
            hits_ref[pl.ds((a * leaves_b + b) * 16, 16)] = jnp.where(
                turned[:16, b : b + 1] == spread, 1.0, 0.0
            ).astype(BF16)

    own_copy.wait()
    for source in (0, 1):
        for ds in (-1, 0, 1):
            for dt in (0, -1, 1):
                ok = exists(-ds, -dt)
                if dt == 1:
                    ok = ok & (core == 0)
                if dt == -1:
                    ok = ok & (core == 1)
                if ds == 0 and dt == 0:
                    ok = core != source

                if dt == 0:
                    for to in (0, 1):

                        @pl.when(ok & (core == to))
                        def _(ds=ds, dt=dt, to=to, source=source):
                            halo_copy(ds, dt, to, source, space, tm, core).wait_recv()
                else:

                    @pl.when(ok)
                    def _(ds=ds, dt=dt, source=source):
                        to = 0 if dt == 1 else 1
                        halo_copy(ds, dt, to, source, space, tm, core).wait_recv()

    row4 = lax.broadcasted_iota(jnp.int32, (4, 1), 0)
    scale = jnp.where(row4 == 2, TIME_SCALE, jnp.where(row4 == 3, 0.0, SPACE_SCALE))
    ones = jnp.where(lax.broadcasted_iota(jnp.int32, (4, 256), 0) < 3, 1.0, 0.0).astype(F32)
    mid_a = (leaves_a + 4) / 2.0 - 0.5
    mid_b = (half + 4) / 2.0 - 0.5

    def features(w, step, carry):
        for part in range(3):
            pair_features(w, step * 3 + part)
        return carry

    def pair_features(w, j):
        tiles = [win[s, w, j].astype(F32) for s in (0, 1)]
        for e in (0, 1):
            slot = (w * win_pairs + j) * 2 + e
            col = (j * 2 + e).astype(F32)
            place = jnp.where(
                row4 == 0,
                (w - mid_a) * CELL,
                jnp.where(row4 == 2, (col - mid_b) * CELL, 0.0),
            )
            at = (tiles[e][8:12] + tiles[e][12:16] + place) * scale
            high, mid, low = split3(at)
            norm = -jnp.sum(at * at, axis=0, keepdims=True)
            norms = jnp.concatenate([*split3(norm), zero1], axis=0)
            feat = jnp.concatenate([high, mid, low, high, mid, high, norms, ones], axis=0)
            other_feat[slot] = feat.astype(BF16)
            probe_rows = jnp.concatenate(
                [tiles[0][4 * e : 4 * e + 4], tiles[1][4 * e : 4 * e + 4]], axis=0
            )
            vectors[slot] = probe_rows.astype(BF16)
            if 2 <= w < 2 + leaves_a:
                norms = jnp.concatenate([*split3(norm + math.log2(0.1)), zero1], axis=0)
                high, mid, low = 2.0 * high, 2.0 * mid, 2.0 * low
                feat = jnp.concatenate([high, high, high, mid, mid, low, ones, norms], axis=0)
                own_feat[(w - 2) * win_pairs * 2 + j * 2 + e] = feat.T.astype(BF16)

    for w in range(leaves_a + 4):
        lax.fori_loop(0, win_pairs // 3, functools.partial(features, w), 0)

    loads["near"].wait()
    picks = near_hbm.shape[2]
    first_a = space * leaves_a - 2
    first_b = tm * leaves_b + core * half - 2

    def near_leaf(i, carry):
        own = own_feat[i // half * (2 * win_pairs) + i % half + 2]
        total = jnp.zeros((own.shape[0], 8), F32)
        for n in range(picks):
            named = near_ref[i // half, core * half + i % half, n]
            slot = (named // columns - first_a) * (half + 4) + named % columns - first_b
            slot = jnp.clip(slot, 0, other_feat.shape[0] - 1)
            kern = jnp.exp2(dot(own, other_feat[slot])).astype(BF16)
            total = total + dot(kern, vectors[slot], NT)
        near_mine[i] = total.T
        return carry

    lax.fori_loop(0, leaves_a * half, near_leaf, 0)

    near_copy = pltpu.make_async_remote_copy(
        src_ref=near_mine,
        dst_ref=near_theirs,
        send_sem=near_ssem,
        recv_sem=near_rsem,
        device_id={"probe": 1 - core},
        device_id_type=MESH,
    )
    near_copy.start()

    own_coef.wait()

    def take_coef(k, carry):
        @pl.when(k != node)
        def _():
            coef_copy(k, k, node).wait_recv()

        return carry

    lax.fori_loop(0, nodes, take_coef, 0)
    hits = hits_ref[...]
    for rp in (0, 1):
        chosen = dot(hits, piece[rp])
        gathered[2 * rp] = chosen[:, :rank].astype(BF16)
        gathered[2 * rp + 1] = chosen[:, rank:].astype(BF16)

    lane = lax.broadcasted_iota(jnp.int32, (rank, 64), 1)
    fold = (
        lax.broadcasted_iota(jnp.int32, (8, 64), 1) // 16
        == lax.broadcasted_iota(jnp.int32, (8, 64), 0)
    ).astype(BF16)

    def couple(blocks, row, length):
        probes4 = jnp.concatenate(
            [gathered[r, pl.ds(row, 16), :] for r in range(4)], axis=0
        )
        full = dot(blocks, probes4, NT)
        total = jnp.zeros((rank, 64), F32)
        for m in range(length):
            total = total + jnp.where(
                lane % 16 == m, full[m * rank : (m + 1) * rank], 0.0
            )
        high = total.astype(BF16)
        low = (total - high.astype(F32)).astype(BF16)
        return dot(fold, high, NT) + dot(fold, low, NT)

    loads["coupling1"].wait()
    loads["coupling0"].wait()
    level_one = couple(
        coupling1_ref[0, 0].reshape(m1 * rank, rank), count * 16, m1
    ).astype(BF16)

    def far_leaves(step, carry):
        a, b = step // (leaves_b // GROUP), step % (leaves_b // GROUP) * GROUP
        totals = [
            couple(
                coupling0[a, b + g].reshape(m0 * rank, rank),
                pl.multiple_of((step * GROUP + g) * 16, 16),
                m0,
            )
            for g in range(GROUP)
        ]
        totals = [
            (totals[g] + dot(level_one, transfer_ref[a, b + g])).astype(BF16)
            for g in range(GROUP)
        ]
        values = [dot(totals[g], basis_ref[a, b + g])[:4] for g in range(GROUP)]
        for g in range(GROUP):
            out_ref[a, b + g] = values[g]
        return carry

    lax.fori_loop(0, count // GROUP, far_leaves, 0)

    near_copy.wait()

    for i in range(leaves_a * half):
        a, b = i // half, i % half
        for refs, at in ((near_mine, core), (near_theirs, 1 - core)):
            value = refs[i]
            value = jnp.where(core == 0, value[:4], value[4:])
            out_ref[a, at * half + b] += value

    for ds, dt, to in halo_pieces():
        ok = exists(ds, dt)
        if ds == 0 and dt == 0:
            ok = core != to

        @pl.when(ok)
        def _(ds=ds, dt=dt, to=to):
            halo_copy(ds, dt, to, core, space + ds, tm + dt, to).wait_send()

    def end_coef(k, carry):
        @pl.when(k != node)
        def _():
            coef_copy(node, k, k).wait_send()

        return carry

    lax.fori_loop(0, nodes, end_coef, 0)


def on_device(
    n_space, n_tm, points, probes, basis, transfer, coupling0, list0, coupling1, list1, near
):
    leaves_a, leaves_b, _, width = points.shape
    rank = basis.shape[2]
    count = leaves_a * leaves_b
    half = leaves_b // 2
    nodes = n_space * n_tm
    args = (points, probes, basis, transfer, coupling0, list0, coupling1, list1, near)
    win_pairs = half // 2 + 2
    window = (leaves_a + 4) * win_pairs * 2
    vmem = pl.BlockSpec(memory_space=pltpu.VMEM)
    return pl.pallas_call(
        functools.partial(kernel, n_space, n_tm),
        out_shape=jax.ShapeDtypeStruct(probes.shape, F32),
        in_specs=[pl.BlockSpec(memory_space=pl.ANY)] * len(args),
        out_specs=vmem,
        scratch_shapes=[pltpu.VMEM(value.shape, value.dtype) for value in args[:-1]]
        + [
            pltpu.SMEM(near.shape, near.dtype),
            pltpu.VMEM((leaves_a, leaves_b // 2, 16, width), BF16),
            pltpu.VMEM((leaves_a + 1, leaves_b, 128), F32),
            pltpu.VMEM(((count + 1) * 16, nodes * NODE_ROWS), BF16),
            pltpu.VMEM((2, leaves_a + 4, win_pairs, 16, width), BF16),
            pltpu.VMEM((window, 32, width), BF16),
            pltpu.VMEM((leaves_a * win_pairs * 2, width, 32), BF16),
            pltpu.VMEM((window, 8, width), BF16),
            pltpu.VMEM((leaves_a * half, 8, width), F32),
            pltpu.VMEM((leaves_a * half, 8, width), F32),
            pltpu.VMEM((2, NODE_ROWS, 2 * rank), F32),
            pltpu.VMEM((2, NODE_ROWS, 2 * rank), BF16),
            pltpu.VMEM((2, nodes * NODE_ROWS, 2 * rank), BF16),
            pltpu.VMEM((4, (count + 1) * 16, rank), BF16),
            pltpu.SemaphoreType.DMA((3, 3, 2)),
            pltpu.SemaphoreType.DMA((2, 3, 3)),
            pltpu.SemaphoreType.DMA((nodes,)),
            pltpu.SemaphoreType.DMA((nodes,)),
            pltpu.SemaphoreType.DMA,
            pltpu.SemaphoreType.DMA,
            pltpu.SemaphoreType.DMA((12,)),
        ],
        compiler_params=pltpu.CompilerParams(
            collective_id=0, has_side_effects=True, vmem_limit_bytes=60 * 1024 * 1024
        ),
    )(*args)


def solution(mesh):
    in_specs = (
        P(("groups", "space"), "tm", None, None),
        P(("groups", "space"), "tm", "probe", None),
        P(("groups", "space"), "tm", None, None),
        P(("groups", "space"), "tm", None, None),
        P(("groups", "space"), "tm", None, None, None),
        P(("groups", "space"), "tm", None),
        P(("groups", "space"), "tm", None, None, None),
        P(("groups", "space"), "tm", None),
        P(("groups", "space"), "tm", None),
    )
    out_specs = P(("groups", "space"), "tm", "probe", None)
    return jax.shard_map(
        functools.partial(on_device, mesh.shape["space"], mesh.shape["tm"]),
        mesh=mesh,
        in_specs=in_specs,
        out_specs=out_specs,
        check_vma=False,
    )
```

```python
import functools
import math

import jax
import jax.numpy as jnp
from jax import lax
from jax.experimental import pallas as pl
from jax.experimental.pallas import tpu as pltpu
from jax.sharding import PartitionSpec as P

CELL = 16
F32 = jnp.float32
BF16 = jnp.bfloat16
MESH = pl.DeviceIdType.MESH
LOG2E = math.log2(math.e)
SPACE_SCALE = math.sqrt(LOG2E / (4.5 * CELL * CELL))
TIME_SCALE = math.sqrt(LOG2E / (2.0 * CELL * CELL))
GROUP = 8
NODE_ROWS = 48

NT = (((1,), (1,)), ((), ()))


def dot(a, b, dims=(((1,), (0,)), ((), ()))):
    return lax.dot_general(a, b, dims, preferred_element_type=F32)


def split3(x):
    high = x.astype(BF16).astype(F32)
    rest = x - high
    mid = rest.astype(BF16).astype(F32)
    return high, mid, rest - mid


def kernel(
    n_space,
    n_tm,
    points_hbm,
    probes_hbm,
    basis_hbm,
    transfer_hbm,
    coupling0_hbm,
    list0_hbm,
    coupling1_hbm,
    list1_hbm,
    near_hbm,
    out_ref,
    points_ref,
    probes_ref,
    basis_ref,
    transfer_ref,
    coupling0,
    list0_ref,
    coupling1_ref,
    list1_ref,
    near_ref,
    pack_ref,
    ids_ref,
    hits_ref,
    win,
    other_feat,
    own_feat,
    vectors,
    near_mine,
    near_theirs,
    coef_f32,
    coef_send,
    piece,
    gathered,
    halo_send,
    halo_recv,
    coef_ssem,
    coef_rsem,
    near_ssem,
    near_rsem,
    local_sem,
):
    space = lax.axis_index("space")
    tm = lax.axis_index("tm")
    core = lax.axis_index("probe")
    node = space * n_tm + tm
    nodes = n_space * n_tm
    leaves_a, leaves_b = basis_ref.shape[0], basis_ref.shape[1]
    count = leaves_a * leaves_b
    half = leaves_b // 2
    pairs = leaves_b // 2
    span = pairs // 2 + 1
    win_pairs = pairs // 2 + 2
    m0 = coupling0_hbm.shape[2]
    m1 = coupling1_ref.shape[2]
    rank = basis_ref.shape[2]

    columns = leaves_b * n_tm
    loads = {}
    for at, (name, source, target) in enumerate(
        (
            ("points", points_hbm, points_ref),
            ("probes", probes_hbm, probes_ref),
            ("basis", basis_hbm, basis_ref),
            ("transfer", transfer_hbm, transfer_ref),
            ("list0", list0_hbm, list0_ref),
            ("list1", list1_hbm, list1_ref),
            ("near", near_hbm, near_ref),
            ("coupling1", coupling1_hbm, coupling1_ref),
            ("coupling0", coupling0_hbm, coupling0),
        )
    ):
        loads[name] = pltpu.make_async_copy(source, target, local_sem.at[at + 3])
        loads[name].start()

    barrier = pltpu.get_barrier_semaphore()

    def greet(k, carry):
        @pl.when(k != node * 2 + core)
        def _():
            pl.semaphore_signal(
                barrier,
                inc=1,
                device_id={
                    "space": k // (2 * n_tm),
                    "tm": (k // 2) % n_tm,
                    "probe": k % 2,
                },
                device_id_type=MESH,
            )

        return carry

    lax.fori_loop(0, 2 * nodes, greet, 0)

    loads["points"].wait()
    loads["probes"].wait()
    row3 = lax.broadcasted_iota(jnp.int32, (3, 1), 0)
    zero1 = jnp.zeros((1, 256), F32)
    for a in range(leaves_a):
        for j in range(pairs):
            east = ((space * leaves_a + a) * CELL + CELL // 2).astype(F32)
            hour = ((tm * leaves_b + 2 * j + core) * CELL + CELL // 2).astype(F32)
            middle = jnp.where(row3 == 0, east, jnp.where(row3 == 2, hour, float(CELL)))
            at = points_ref[a, 2 * j + core] - middle
            high = at.astype(BF16).astype(F32)
            tile = jnp.concatenate(
                [
                    probes_ref[a, 2 * j].astype(F32),
                    probes_ref[a, 2 * j + 1].astype(F32),
                    high,
                    zero1,
                    at - high,
                    zero1,
                ],
                axis=0,
            )
            pack_ref[a, j] = tile.astype(BF16)
    pl.semaphore_wait(barrier, 2 * nodes - 1)

    def halo_pieces():
        for ds in (-1, 0, 1):
            for dt in (0, -1, 1):
                for to in (0, 1):
                    if dt == 1 and to == 1 or dt == -1 and to == 0:
                        continue
                    yield ds, dt, to

    def exists(ds, dt):
        s, t = space + ds, tm + dt
        return (s >= 0) & (s < n_space) & (t >= 0) & (t < n_tm)

    def halo_copy(ds, dt, to, source, s, t, c):
        if dt == 0:
            first, slot, length = 3 * to, 1 - to, span
        elif dt == 1:
            first, slot, length = pairs - 1, 0, 1
        else:
            first, slot, length = 0, win_pairs - 1, 1
        if dt == 0:
            first = (pairs // 2 - 1) * to
        return pltpu.make_async_remote_copy(
            src_ref=pack_ref.at[:, pl.ds(first, length)],
            dst_ref=win.at[source, pl.ds(2 - 2 * ds, 2), pl.ds(slot, length)],
            send_sem=halo_send.at[ds + 1, dt + 1, to],
            recv_sem=halo_recv.at[source, ds + 1, dt + 1],
            device_id={"space": s, "tm": t, "probe": c},
            device_id_type=MESH,
        )

    own_first = (pairs // 2 - 1) * core
    own_copy = pltpu.make_async_copy(
        pack_ref.at[:, pl.ds(own_first, span)],
        win.at[core, pl.ds(2, 2), pl.ds(1 - core, span)],
        local_sem.at[1],
    )
    own_copy.start()
    for ds, dt, to in halo_pieces():
        ok = exists(ds, dt)
        if ds == 0 and dt == 0:
            ok = core != to

        @pl.when(ok)
        def _(ds=ds, dt=dt, to=to):
            halo_copy(ds, dt, to, core, space + ds, tm + dt, to).start()

    loads["basis"].wait()
    loads["transfer"].wait()
    node_sum = jnp.zeros((4, rank), F32)
    for i in range(count):
        a, b = i // leaves_b, i % leaves_b
        value = dot(probes_ref[a, b], basis_ref[a, b], NT).astype(BF16)
        node_sum = node_sum + dot(value, transfer_ref[a, b], NT)
        value = value.astype(F32)
        for r in range(4):
            coef_f32[r // 2, i, pl.ds((r % 2) * rank, rank)] = value[r]
    node_sum = node_sum.astype(BF16).astype(F32)
    for r in range(4):
        coef_f32[r // 2, count, pl.ds((r % 2) * rank, rank)] = node_sum[r]
    coef_f32[:, pl.ds(count + 1, NODE_ROWS - count - 1)] = jnp.zeros(
        (2, NODE_ROWS - count - 1, 2 * rank), F32
    )
    coef_send[...] = coef_f32[...].astype(BF16)

    def coef_copy(at, sem_at, to):
        return pltpu.make_async_remote_copy(
            src_ref=coef_send,
            dst_ref=piece.at[:, pl.ds(pl.multiple_of(at * NODE_ROWS, 16), NODE_ROWS)],
            send_sem=coef_ssem.at[sem_at],
            recv_sem=coef_rsem.at[at],
            device_id={"space": to // n_tm, "tm": to % n_tm, "probe": core},
            device_id_type=MESH,
        )

    def send_coef(k, carry):
        @pl.when(k != node)
        def _():
            coef_copy(node, k, k).start()

        return carry

    lax.fori_loop(0, nodes, send_coef, 0)
    own_coef = pltpu.make_async_copy(
        coef_send,
        piece.at[:, pl.ds(pl.multiple_of(node * NODE_ROWS, 16), NODE_ROWS)],
        local_sem.at[2],
    )
    own_coef.start()

    loads["list0"].wait()
    loads["list1"].wait()
    ids_ref[...] = jnp.full(ids_ref.shape, -1.0, F32)
    for a in range(leaves_a):
        named = list0_ref[a]
        row, column = named // columns, named % columns
        place = (
            (row // leaves_a * n_tm + column // leaves_b) * NODE_ROWS
            + row % leaves_a * leaves_b
            + column % leaves_b
        )
        ids_ref[a, :, pl.ds(0, m0)] = jnp.where(named < 0, -1, place).astype(F32)
    named = list1_ref[0]
    ids_ref[leaves_a, pl.ds(0, 1), pl.ds(0, m1)] = jnp.where(
        named < 0, -1, named * NODE_ROWS + count
    ).astype(F32)
    spread = lax.broadcasted_iota(jnp.int32, (16, nodes * NODE_ROWS), 1).astype(F32)
    for a in range(leaves_a + 1):
        turned = ids_ref[a].T
        for b in range(leaves_b if a < leaves_a else 1):
            hits_ref[pl.ds((a * leaves_b + b) * 16, 16)] = jnp.where(
                turned[:16, b : b + 1] == spread, 1.0, 0.0
            ).astype(BF16)

    own_copy.wait()
    for source in (0, 1):
        for ds in (-1, 0, 1):
            for dt in (0, -1, 1):
                ok = exists(-ds, -dt)
                if dt == 1:
                    ok = ok & (core == 0)
                if dt == -1:
                    ok = ok & (core == 1)
                if ds == 0 and dt == 0:
                    ok = core != source

                if dt == 0:
                    for to in (0, 1):

                        @pl.when(ok & (core == to))
                        def _(ds=ds, dt=dt, to=to, source=source):
                            halo_copy(ds, dt, to, source, space, tm, core).wait_recv()
                else:

                    @pl.when(ok)
                    def _(ds=ds, dt=dt, source=source):
                        to = 0 if dt == 1 else 1
                        halo_copy(ds, dt, to, source, space, tm, core).wait_recv()

    row4 = lax.broadcasted_iota(jnp.int32, (4, 1), 0)
    scale = jnp.where(row4 == 2, TIME_SCALE, jnp.where(row4 == 3, 0.0, SPACE_SCALE))
    ones = jnp.where(lax.broadcasted_iota(jnp.int32, (4, 256), 0) < 3, 1.0, 0.0).astype(F32)
    mid_a = (leaves_a + 4) / 2.0 - 0.5
    mid_b = (half + 4) / 2.0 - 0.5

    def features(w, step, carry):
        for part in range(3):
            pair_features(w, step * 3 + part)
        return carry

    def pair_features(w, j):
        tiles = [win[s, w, j].astype(F32) for s in (0, 1)]
        for e in (0, 1):
            slot = (w * win_pairs + j) * 2 + e
            col = (j * 2 + e).astype(F32)
            place = jnp.where(
                row4 == 0,
                (w - mid_a) * CELL,
                jnp.where(row4 == 2, (col - mid_b) * CELL, 0.0),
            )
            at = (tiles[e][8:12] + tiles[e][12:16] + place) * scale
            high, mid, low = split3(at)
            norm = -jnp.sum(at * at, axis=0, keepdims=True)
            norms = jnp.concatenate([*split3(norm), zero1], axis=0)
            feat = jnp.concatenate([high, mid, low, high, mid, high, norms, ones], axis=0)
            other_feat[slot] = feat.astype(BF16)
            probe_rows = jnp.concatenate(
                [tiles[0][4 * e : 4 * e + 4], tiles[1][4 * e : 4 * e + 4]], axis=0
            )
            vectors[slot] = probe_rows.astype(BF16)
            if 2 <= w < 2 + leaves_a:
                norms = jnp.concatenate([*split3(norm + math.log2(0.1)), zero1], axis=0)
                high, mid, low = 2.0 * high, 2.0 * mid, 2.0 * low
                feat = jnp.concatenate([high, high, high, mid, mid, low, ones, norms], axis=0)
                own_feat[(w - 2) * win_pairs * 2 + j * 2 + e] = feat.T.astype(BF16)

    for w in range(leaves_a + 4):
        lax.fori_loop(0, win_pairs // 3, functools.partial(features, w), 0)

    loads["near"].wait()
    picks = near_hbm.shape[2]
    first_a = space * leaves_a - 2
    first_b = tm * leaves_b + core * half - 2

    def near_leaf(i, carry):
        own = own_feat[i // half * (2 * win_pairs) + i % half + 2]
        total = jnp.zeros((8, own.shape[0]), F32)
        for n in range(picks):
            named = near_ref[i // half, core * half + i % half, n]
            slot = (named // columns - first_a) * (half + 4) + named % columns - first_b
            slot = jnp.clip(slot, 0, other_feat.shape[0] - 1)
            kern = jnp.exp2(dot(own, other_feat[slot])).astype(BF16)
            total = total + dot(vectors[slot], kern, NT)
        near_mine[i] = total
        return carry

    lax.fori_loop(0, leaves_a * half, near_leaf, 0)

    near_copy = pltpu.make_async_remote_copy(
        src_ref=near_mine,
        dst_ref=near_theirs,
        send_sem=near_ssem,
        recv_sem=near_rsem,
        device_id={"probe": 1 - core},
        device_id_type=MESH,
    )
    near_copy.start()

    own_coef.wait()

    def take_coef(k, carry):
        @pl.when(k != node)
        def _():
            coef_copy(k, k, node).wait_recv()

        return carry

    lax.fori_loop(0, nodes, take_coef, 0)
    hits = hits_ref[...]
    for rp in (0, 1):
        chosen = dot(hits, piece[rp])
        gathered[2 * rp] = chosen[:, :rank].astype(BF16)
        gathered[2 * rp + 1] = chosen[:, rank:].astype(BF16)

    lane = lax.broadcasted_iota(jnp.int32, (rank, 64), 1)
    fold = (
        lax.broadcasted_iota(jnp.int32, (8, 64), 1) // 16
        == lax.broadcasted_iota(jnp.int32, (8, 64), 0)
    ).astype(BF16)

    def couple(blocks, row, length):
        probes4 = jnp.concatenate(
            [gathered[r, pl.ds(row, 16), :] for r in range(4)], axis=0
        )
        full = dot(blocks, probes4, NT)
        total = jnp.zeros((rank, 64), F32)
        for m in range(length):
            total = total + jnp.where(
                lane % 16 == m, full[m * rank : (m + 1) * rank], 0.0
            )
        high = total.astype(BF16)
        low = (total - high.astype(F32)).astype(BF16)
        return dot(fold, high, NT) + dot(fold, low, NT)

    loads["coupling1"].wait()
    loads["coupling0"].wait()
    level_one = couple(
        coupling1_ref[0, 0].reshape(m1 * rank, rank), count * 16, m1
    ).astype(BF16)

    def far_leaves(step, carry):
        a, b = step // (leaves_b // GROUP), step % (leaves_b // GROUP) * GROUP
        totals = [
            couple(
                coupling0[a, b + g].reshape(m0 * rank, rank),
                pl.multiple_of((step * GROUP + g) * 16, 16),
                m0,
            )
            for g in range(GROUP)
        ]
        totals = [
            (totals[g] + dot(level_one, transfer_ref[a, b + g])).astype(BF16)
            for g in range(GROUP)
        ]
        values = [dot(totals[g], basis_ref[a, b + g])[:4] for g in range(GROUP)]
        for g in range(GROUP):
            out_ref[a, b + g] = values[g]
        return carry

    lax.fori_loop(0, count // GROUP, far_leaves, 0)

    near_copy.wait()

    for i in range(leaves_a * half):
        a, b = i // half, i % half
        for refs, at in ((near_mine, core), (near_theirs, 1 - core)):
            value = refs[i]
            value = jnp.where(core == 0, value[:4], value[4:])
            out_ref[a, at * half + b] += value

    for ds, dt, to in halo_pieces():
        ok = exists(ds, dt)
        if ds == 0 and dt == 0:
            ok = core != to

        @pl.when(ok)
        def _(ds=ds, dt=dt, to=to):
            halo_copy(ds, dt, to, core, space + ds, tm + dt, to).wait_send()

    def end_coef(k, carry):
        @pl.when(k != node)
        def _():
            coef_copy(node, k, k).wait_send()

        return carry

    lax.fori_loop(0, nodes, end_coef, 0)


def on_device(
    n_space, n_tm, points, probes, basis, transfer, coupling0, list0, coupling1, list1, near
):
    leaves_a, leaves_b, _, width = points.shape
    rank = basis.shape[2]
    count = leaves_a * leaves_b
    half = leaves_b // 2
    nodes = n_space * n_tm
    args = (points, probes, basis, transfer, coupling0, list0, coupling1, list1, near)
    win_pairs = half // 2 + 2
    window = (leaves_a + 4) * win_pairs * 2
    vmem = pl.BlockSpec(memory_space=pltpu.VMEM)
    return pl.pallas_call(
        functools.partial(kernel, n_space, n_tm),
        out_shape=jax.ShapeDtypeStruct(probes.shape, F32),
        in_specs=[pl.BlockSpec(memory_space=pl.ANY)] * len(args),
        out_specs=vmem,
        scratch_shapes=[pltpu.VMEM(value.shape, value.dtype) for value in args[:-1]]
        + [
            pltpu.SMEM(near.shape, near.dtype),
            pltpu.VMEM((leaves_a, leaves_b // 2, 16, width), BF16),
            pltpu.VMEM((leaves_a + 1, leaves_b, 128), F32),
            pltpu.VMEM(((count + 1) * 16, nodes * NODE_ROWS), BF16),
            pltpu.VMEM((2, leaves_a + 4, win_pairs, 16, width), BF16),
            pltpu.VMEM((window, 32, width), BF16),
            pltpu.VMEM((leaves_a * win_pairs * 2, width, 32), BF16),
            pltpu.VMEM((window, 8, width), BF16),
            pltpu.VMEM((leaves_a * half, 8, width), F32),
            pltpu.VMEM((leaves_a * half, 8, width), F32),
            pltpu.VMEM((2, NODE_ROWS, 2 * rank), F32),
            pltpu.VMEM((2, NODE_ROWS, 2 * rank), BF16),
            pltpu.VMEM((2, nodes * NODE_ROWS, 2 * rank), BF16),
            pltpu.VMEM((4, (count + 1) * 16, rank), BF16),
            pltpu.SemaphoreType.DMA((3, 3, 2)),
            pltpu.SemaphoreType.DMA((2, 3, 3)),
            pltpu.SemaphoreType.DMA((nodes,)),
            pltpu.SemaphoreType.DMA((nodes,)),
            pltpu.SemaphoreType.DMA,
            pltpu.SemaphoreType.DMA,
            pltpu.SemaphoreType.DMA((12,)),
        ],
        compiler_params=pltpu.CompilerParams(
            collective_id=0, has_side_effects=True, vmem_limit_bytes=60 * 1024 * 1024
        ),
    )(*args)


def solution(mesh):
    in_specs = (
        P(("groups", "space"), "tm", None, None),
        P(("groups", "space"), "tm", "probe", None),
        P(("groups", "space"), "tm", None, None),
        P(("groups", "space"), "tm", None, None),
        P(("groups", "space"), "tm", None, None, None),
        P(("groups", "space"), "tm", None),
        P(("groups", "space"), "tm", None, None, None),
        P(("groups", "space"), "tm", None),
        P(("groups", "space"), "tm", None),
    )
    out_specs = P(("groups", "space"), "tm", "probe", None)
    return jax.shard_map(
        functools.partial(on_device, mesh.shape["space"], mesh.shape["tm"]),
        mesh=mesh,
        in_specs=in_specs,
        out_specs=out_specs,
        check_vma=False,
    )
```
